256 devices in a mesh: pts: 16 (over x_hi, z), fn: 16 (over x_lo, y, core).
Axes of the slice: x: 4 (x_hi: 2, x_lo: 2; x = x_hi * 2 + x_lo), y: 4, z: 8, core: 2. Of those that a mesh axis runs over, the one named last changes fastest.
Arguments:
- grad_out: bfloat16 [128, 131072], P('fn', 'pts'), may hold values from -0.0390625 to 0.0390625
- coef: bfloat16 [128, 512], P('fn'), may hold values from -0.5 to 0.5
- coords: float32 [3, 131072], P(None, 'pts'), may hold values from -1 to 1
- w_first: float32 [3, 512], replicated, may hold values from -3.5 to 3.5
- b_first: float32 [512], replicated, may hold values from -3 to 3
- w_second: bfloat16 [512, 512], replicated, may hold values from -0.25 to 0.25
- b_second: float32 [512], replicated, may hold values from -3 to 3
- w_third: bfloat16 [512, 512], replicated, may hold values from -0.25 to 0.25
- b_third: float32 [512], replicated, may hold values from -4 to 4
Outputs:
- grad_coef: float32 [128, 512], P('fn', 'pts')
- grad_w_first: float32 [3, 512], replicated
- grad_b_first: float32 [512], replicated
- grad_w_second: float32 [512, 512], replicated
- grad_b_second: float32 [512], replicated
- grad_w_third: float32 [512, 512], replicated
- grad_b_third: float32 [512], replicated
The draws below stay inside these ranges and needn't reach their ends.
All inputs are finite; a program needn't handle non-finite values.
Results may differ from the reference program's by a relative error of at most 0.012.
The reference program's roundings to bfloat16 on the way (of `act_one`, `act_two`, `basis`, `grad_basis` and `pre_two`) count: a program that leaves them out, or rounds other values in their place, can miss the bound.
Values may be sent and summed in bfloat16 or wider, within the bound.
No kernel may reach another device: no remote copies, remote signals or barrier semaphores. Data moves between devices by JAX's collectives and lax.ppermute only.
A program may use at most 128 MiB of HBM per device.

```python
import jax
import jax.numpy as jnp
from jax import lax

H = 512
P_SIZE = 512
F = 128
X = 131072


def draw_w_first(key, part):
    key = jax.random.fold_in(key, 11)
    return jax.random.uniform(key, (3, H), jnp.float32, -3.5, 3.5)


def draw_w_second(key, part):
    key = jax.random.fold_in(key, 23)
    values = jax.random.uniform(key, (H, H), jnp.float32, -0.25, 0.25)
    return values.astype(jnp.bfloat16)


def shard_levels(own_key, extent, shards, low, top_value):
    level, own = 1.0, jax.random.fold_in(own_key, 6)
    for axis_at, blocks in shards:
        steps = jnp.exp(jax.random.uniform(jax.random.fold_in(own, axis_at), (blocks,), jnp.float32, low / len(shards), top_value / len(shards)))
        level = level * jnp.repeat(steps, extent[axis_at] // blocks).reshape([-1 if axis == axis_at else 1 for axis in range(len(extent))])
    return level


def gaussian(own_key, shape, scale, bound, shards=(), held_as=jnp.bfloat16):
    factor_of = shard_levels(own_key, shape, shards, -0.22, 0.18) if shards else 1.0
    entries = jax.random.normal(own_key, shape, jnp.float32) * scale * factor_of
    return jnp.minimum(jnp.maximum(entries, -bound), bound).astype(held_as)


def setup_inputs(seed: int = 0) -> dict:
    seeds = jax.random.split(jax.random.key(seed), 10)
    return {
        "grad_out": gaussian(seeds[0], (F, X), (X ** -0.5), 0.0390625, ((0, 16), (1, 16))),
        "coef": gaussian(seeds[1], (F, P_SIZE), F ** -0.5, 0.5, ((0, 16),)),
        "coords": jnp.clip(jax.random.uniform(seeds[2], (3, X), jnp.float32, -1.0, 1.0) * shard_levels(seeds[2], (3, X), ((1, 16),), -0.4, 0.0), -1.0, 1.0),
        "w_first": draw_w_first(jax.random.fold_in(seeds[9], 71), 0),
        "b_first": jnp.clip(jax.random.uniform(seeds[4], (H,), jnp.float32, -3.0, 3.0), -3.0, 3.0),
        "w_second": draw_w_second(jax.random.fold_in(seeds[9], 71), 0),
        "b_second": gaussian(seeds[6], (H,), 0.5, 3.0, (), jnp.float32),
        "w_third": gaussian(seeds[7], (H, P_SIZE), H ** -0.5, 0.25),
        "b_third": gaussian(seeds[8], (P_SIZE,), 1.0, 4.0, (), jnp.float32),
    }


def reference(grad_out, coef, coords, w_first, b_first, w_second, b_second, w_third, b_third):
    high = lax.Precision.HIGHEST
    z_one = jnp.dot(coords.T, w_first, precision=high, preferred_element_type=jnp.float32) + b_first
    act_one = jnp.tanh(z_one).astype(jnp.bfloat16)
    act_two = jnp.tanh(jnp.dot(act_one, w_second, preferred_element_type=jnp.float32) + b_second).astype(jnp.bfloat16)
    basis = (jnp.dot(act_two, w_third, preferred_element_type=jnp.float32) + b_third).astype(jnp.bfloat16)
    grad_coef = jnp.dot(grad_out, basis, preferred_element_type=jnp.float32)
    grad_basis = jnp.dot(grad_out.T, coef, preferred_element_type=jnp.float32).astype(jnp.bfloat16)
    grad_w_third = jnp.dot(act_two.T, grad_basis, preferred_element_type=jnp.float32)
    grad_b_third = jnp.sum(grad_basis.astype(jnp.float32), axis=0)
    two_f = act_two.astype(jnp.float32)
    pre_two = (jnp.dot(grad_basis, w_third.T, preferred_element_type=jnp.float32) * (1.0 - two_f * two_f)).astype(jnp.bfloat16)
    grad_w_second = jnp.dot(act_one.T, pre_two, preferred_element_type=jnp.float32)
    grad_b_second = jnp.sum(pre_two.astype(jnp.float32), axis=0)
    one_f = act_one.astype(jnp.float32)
    pre_one = jnp.dot(pre_two, w_second.T, preferred_element_type=jnp.float32) * (1.0 - one_f * one_f)
    grad_w_first = jnp.dot(coords, pre_one, precision=high, preferred_element_type=jnp.float32)
    grad_b_first = jnp.sum(pre_one, axis=0)
    return grad_coef, grad_w_first, grad_b_first, grad_w_second, grad_b_second, grad_w_third, grad_b_third
```

```python
import jax
import jax.numpy as jnp
from jax import lax
from jax.experimental import pallas as pl
from jax.experimental.pallas import tpu as pltpu
from jax.sharding import Mesh, PartitionSpec as P

SPLIT = (("xh", 2), ("z", 8), ("xl", 2), ("y", 4), ("c", 2))
AXES = tuple(name for name, _ in SPLIT)
SIZES = tuple(size for _, size in SPLIT)
PLANE = ("xh", "xl", "y")
VMEM_BYTES = 48 * 1024 * 1024
BF16, F32 = jnp.bfloat16, jnp.float32


def nn(a, b):
    return lax.dot_general(a, b, (((1,), (0,)), ((), ())), preferred_element_type=F32)


def nt(a, b):
    return lax.dot_general(a, b, (((1,), (1,)), ((), ())), preferred_element_type=F32)


def tn(a, b):
    return lax.dot_general(a, b, (((0,), (0,)), ((), ())), preferred_element_type=F32)


def fold(a):
    return jnp.concatenate([a[:, :128], a[:, 128:]], axis=0)


def compute_kernel(
    place_ref, recv_ref, coords_ref, w_first_ref, b_first_ref, w_second_ref, b_second_ref,
    w_third_ref, b_third_ref, out_ref, one_ref, two_ref, grad_basis_ref, pre_two_ref, coef_ref,
):
    core, block = place_ref[0], place_ref[1]
    points = one_ref.shape[1]
    half = w_second_ref.shape[0] // 2
    own = pl.ds(pl.multiple_of(core * half, half), half)
    xyz = coords_ref[:, pl.ds(pl.multiple_of(block * points, points), points)]
    w_one = w_first_ref[...].T
    z_one = w_one[:, 0:1] * xyz[0:1] + w_one[:, 1:2] * xyz[1:2] + w_one[:, 2:3] * xyz[2:3]
    one_ref[...] = jnp.tanh(z_one + b_first_ref[...].T).astype(BF16)
    two_ref[...] = jnp.tanh(tn(w_second_ref[...], one_ref[...]) + b_second_ref[...].T).astype(BF16)
    basis = (tn(w_third_ref[...], two_ref[...]) + b_third_ref[...].T).astype(BF16)

    grads = recv_ref[:, :points]
    coef_ref[...] = nt(grads, basis)
    grad_basis_ref[...] = tn(recv_ref[:, points:], grads).astype(BF16)
    out_ref[:, :16, :512] = nt(two_ref[own, :], grad_basis_ref[...]).astype(BF16).reshape(16, 16, 512)
    two = two_ref[...].astype(F32)
    pre_two_ref[...] = (nn(w_third_ref[...], grad_basis_ref[...]) * (1.0 - two * two)).astype(BF16)
    out_ref[:, 16:, :512] = nt(one_ref[own, :], pre_two_ref[...]).astype(BF16).reshape(16, 16, 512)
    one = one_ref[own, :].astype(F32)
    pre_one = nn(w_second_ref[own, :], pre_two_ref[...]) * (1.0 - one * one)

    ones = jnp.ones((8, points), BF16)
    xyz_hi = xyz.astype(BF16)
    rest = xyz - xyz_hi.astype(F32)
    xyz_mid = rest.astype(BF16)
    xyz_lo = rest - xyz_mid.astype(F32)
    rows = jnp.concatenate(
        [xyz_hi.astype(F32), xyz_mid.astype(F32), xyz_lo, jnp.ones((7, points), F32)], axis=0
    ).astype(BF16)
    pre_hi = pre_one.astype(BF16)
    pre_rest = pre_one - pre_hi.astype(F32)
    pre_mid = pre_rest.astype(BF16)
    pre_lo = (pre_rest - pre_mid.astype(F32)).astype(BF16)
    terms = nt(rows, pre_hi) + nt(rows, pre_mid) + nt(rows, pre_lo)
    grad_w_first = terms[0:3] + terms[3:6] + terms[6:9]
    small = jnp.concatenate(
        [
            grad_w_first,
            terms[9:10],
            nt(ones, pre_two_ref[own, :])[0:1],
            nt(ones, grad_basis_ref[own, :])[0:1],
            jnp.zeros((2, half), F32),
        ],
        axis=0,
    )
    out_ref[0, 16:, 512:] = fold(small).astype(BF16)
    for at in range(16):
        if at:
            out_ref[at, 16:, 512:] = jnp.zeros((16, 128), BF16)
        group, column = at % 8, at // 8
        mine = coef_ref[pl.ds(pl.multiple_of(group * 16 + core * 8, 8), 8), column * half : column * half + half]
        out_ref[at, :16, 512:] = fold(mine).astype(BF16)


def finish_kernel(core_ref, own_ref, other_ref, w_first_ref, b_first_ref, w_second_ref, b_second_ref, w_third_ref, b_third_ref):
    half = 256
    for at, ref in ((core_ref[0], own_ref), (1 - core_ref[0], other_ref)):
        where = pl.ds(pl.multiple_of(at * half, half), half)
        w_third_ref[where, :] = ref[:, :16, :512].reshape(half, 512).astype(F32)
        w_second_ref[where, :] = ref[:, 16:, :512].reshape(half, 512).astype(F32)
        small = ref[0, 16:, 512:].astype(F32)
        small = jnp.concatenate([small[:8], small[8:]], axis=1)
        w_first_ref[:, where] = small[0:3]
        b_first_ref[:, where] = small[3:4]
        b_second_ref[:, where] = small[4:5]
        b_third_ref[:, where] = small[5:6]


def swap(value, flip):
    axis, bits = flip
    return lax.ppermute(value, axis, [(i, i ^ bits) for i in range(dict(SPLIT)[axis])])


def shards(grad_out, coef, coords, w_first, b_first, w_second, b_second, w_third, b_third):
    xl, y, core = lax.axis_index("xl"), lax.axis_index("y"), lax.axis_index("c")
    points = grad_out.shape[1] // 8
    smem = pl.BlockSpec(memory_space=pltpu.SMEM)
    vmem = pl.BlockSpec(memory_space=pltpu.VMEM)

    blocks = grad_out.reshape(8, 8, points).transpose(1, 0, 2)
    send = jnp.concatenate([blocks, jnp.broadcast_to(coef, (8, *coef.shape))], axis=2)
    send = jnp.broadcast_to(send[:, None], (8, 2, *send.shape[1:])).reshape(16, 8, points + 512)
    recv = lax.all_to_all(send, ("xl", "y", "c"), 0, 0, tiled=True).reshape(128, points + 512)

    place = jnp.stack([core, xl * 4 + y]).astype(jnp.int32)
    partial = pl.pallas_call(
        compute_kernel,
        out_shape=jax.ShapeDtypeStruct((16, 32, 640), BF16),
        in_specs=[smem] + [vmem] * 8,
        out_specs=vmem,
        scratch_shapes=[pltpu.VMEM((512, points), BF16)] * 4 + [pltpu.VMEM((128, 512), F32)],
        compiler_params=pltpu.CompilerParams(vmem_limit_bytes=VMEM_BYTES),
    )(place, recv, coords, w_first, b_first[None], w_second, b_second[None], w_third, b_third[None])

    parts = lax.all_to_all(partial, PLANE, 0, 0, tiled=True)
    mine = jnp.sum(parts.astype(F32), axis=0).astype(BF16)
    one, two, three = (swap(mine, ("z", bits)).astype(F32) for bits in (1, 2, 3))
    mine = ((mine.astype(F32) + one) + (two + three)).astype(BF16)
    mine = (mine.astype(F32) + swap(mine, ("z", 7)).astype(F32)).astype(BF16)

    gathered = lax.all_to_all(jnp.broadcast_to(mine, (16, 32, 640)), PLANE, 0, 0, tiled=True)
    other = swap(gathered, ("c", 1))
    own_coef = mine[:16, 512:].astype(F32)
    own_coef = jnp.concatenate([own_coef[:8], own_coef[8:]], axis=1)
    grad_coef = lax.dynamic_slice_in_dim(own_coef, lax.axis_index("z") * 32, 32, 1)

    row = jax.ShapeDtypeStruct((1, 512), F32)
    square = jax.ShapeDtypeStruct((512, 512), F32)
    w_one, b_one, w_two, b_two, w_three, b_three = pl.pallas_call(
        finish_kernel,
        out_shape=(jax.ShapeDtypeStruct((3, 512), F32), row, square, row, square, row),
        in_specs=[smem, vmem, vmem],
        out_specs=(vmem,) * 6,
        compiler_params=pltpu.CompilerParams(vmem_limit_bytes=VMEM_BYTES),
    )(place[:1], gathered, other)
    return (grad_coef, w_one, b_one[0], w_two, b_two[0], w_three, b_three[0])


def solution(mesh):
    fine = Mesh(mesh.devices.reshape(SIZES), AXES)
    fn, pts = ("xl", "y", "c"), ("xh", "z")
    return jax.shard_map(
        shards,
        mesh=fine,
        in_specs=(P(fn, pts), P(fn, None), P(None, pts), P(), P(), P(), P(), P(), P()),
        out_specs=(P(fn, pts), P(), P(), P(), P(), P(), P()),
        check_vma=False,
    )
```

```python
import jax
import jax.numpy as jnp
from jax import lax
from jax.experimental import pallas as pl
from jax.experimental.pallas import tpu as pltpu
from jax.sharding import Mesh, PartitionSpec as P

SPLIT = (("xh", 2), ("z", 8), ("xl", 2), ("y", 4), ("c", 2))
AXES = tuple(name for name, _ in SPLIT)
SIZES = tuple(size for _, size in SPLIT)
PLANE = ("xh", "xl", "y")
VMEM_BYTES = 20 * 1024 * 1024
BF16, F32 = jnp.bfloat16, jnp.float32


def nn(a, b):
    return lax.dot_general(a, b, (((1,), (0,)), ((), ())), preferred_element_type=F32)


def nt(a, b):
    return lax.dot_general(a, b, (((1,), (1,)), ((), ())), preferred_element_type=F32)


def tn(a, b):
    return lax.dot_general(a, b, (((0,), (0,)), ((), ())), preferred_element_type=F32)


def fold(a):
    return jnp.concatenate([a[:, :128], a[:, 128:]], axis=0)


def across(a):
    total = a[:, :128]
    for at in range(128, a.shape[1], 128):
        total = total + a[:, at : at + 128]
    return jnp.sum(total.T, axis=0, keepdims=True)


def unfold(a):
    return jnp.concatenate([a[:8], a[8:]], axis=1)


def pack_kernel(grad_out_ref, coef_ref, out_ref):
    blocks, rows, width = out_ref.shape
    points = width - coef_ref.shape[1]
    for at in range(blocks):
        out_ref[at, :, :points] = grad_out_ref[:, at * points : (at + 1) * points]
        out_ref[at, :, points:] = coef_ref[...]


def forward_kernel(
    coords_ref, w_first_ref, b_first_ref, w_second_ref, b_second_ref, w_third_ref, b_third_ref,
    acts_ref, basis_ref, xyz_ref, small_ref, bias_ref, weights_ref, sems,
):
    one_ref, two_ref = acts_ref.at[0], acts_ref.at[1]
    points = one_ref.shape[1]
    at = lax.axis_index("xl") * 4 + lax.axis_index("y")
    block = pl.ds(pl.multiple_of(at * points, points), points)
    copies = [
        pltpu.make_async_copy(coords_ref.at[:, block], xyz_ref, sems.at[0]),
        pltpu.make_async_copy(w_first_ref, small_ref, sems.at[1]),
        pltpu.make_async_copy(b_first_ref, bias_ref.at[0], sems.at[2]),
        pltpu.make_async_copy(b_second_ref, bias_ref.at[1], sems.at[3]),
        pltpu.make_async_copy(b_third_ref, bias_ref.at[2], sems.at[4]),
        pltpu.make_async_copy(w_second_ref, weights_ref.at[0], sems.at[5]),
        pltpu.make_async_copy(w_third_ref, weights_ref.at[1], sems.at[6]),
    ]
    for copy in copies:
        copy.start()
    for copy in copies[:5]:
        copy.wait()
    xyz = xyz_ref[...]
    w_one = small_ref[...].T
    z_one = w_one[:, 0:1] * xyz[0:1] + w_one[:, 1:2] * xyz[1:2] + w_one[:, 2:3] * xyz[2:3]
    one_ref[...] = jnp.tanh(z_one + bias_ref[0].T).astype(BF16)
    copies[5].wait()
    two_ref[...] = jnp.tanh(tn(weights_ref[0], one_ref[...]) + bias_ref[1].T).astype(BF16)
    copies[6].wait()
    basis_ref[...] = (tn(weights_ref[1], two_ref[...]) + bias_ref[2].T).astype(BF16)


def middle_kernel(near_ref, basis_ref, w_second_ref, w_third_ref, coef_ref, weights_ref, sems):
    copies = [
        pltpu.make_async_copy(w_second_ref, weights_ref.at[0], sems.at[0]),
        pltpu.make_async_copy(w_third_ref, weights_ref.at[1], sems.at[1]),
    ]
    for copy in copies:
        copy.start()
    coef_ref[...] = nt(near_ref[:, : basis_ref.shape[1]], basis_ref[...])
    for copy in copies:
        copy.wait()


def backward_kernel(
    near_ref, far_ref, xyz_ref, weights_ref, coef_ref, acts_ref, out_ref, grad_basis_ref, pre_two_ref
):
    one_ref, two_ref = acts_ref.at[0], acts_ref.at[1]
    w_second_ref, w_third_ref = weights_ref.at[0], weights_ref.at[1]
    core = lax.axis_index("c")
    points = one_ref.shape[1]
    half = w_second_ref.shape[0] // 2
    own = pl.ds(pl.multiple_of(core * half, half), half)
    grad_basis = tn(near_ref[:, points:], near_ref[:, :points])
    grad_basis = grad_basis + tn(far_ref[:, points:], far_ref[:, :points])
    grad_basis_ref[...] = grad_basis.astype(BF16)
    out_ref[:, :16, :512] = nt(two_ref[own, :], grad_basis_ref[...]).astype(BF16).reshape(16, 16, 512)
    two = two_ref[...].astype(F32)
    pre_two_ref[...] = (nn(w_third_ref[...], grad_basis_ref[...]) * (1.0 - two * two)).astype(BF16)
    out_ref[:, 16:, :512] = nt(one_ref[own, :], pre_two_ref[...]).astype(BF16).reshape(16, 16, 512)
    one = one_ref[own, :].astype(F32)
    pre_one = nn(w_second_ref[own, :], pre_two_ref[...]) * (1.0 - one * one)

    xyz = xyz_ref[...]
    small = [across(pre_one * xyz[axis : axis + 1]) for axis in range(3)]
    small += [across(pre_one), across(pre_two_ref[own, :].astype(F32))]
    small += [across(grad_basis_ref[own, :].astype(F32)), jnp.zeros((2, half), F32)]
    small = fold(jnp.concatenate(small, axis=0)).astype(BF16)
    for at in range(16):
        group, column = at % 8, at // 8
        mine = coef_ref[group * 8 : group * 8 + 8, column * half : column * half + half]
        out_ref[at, :16, 512:] = fold(mine).astype(BF16)
        out_ref[at, 16:, 512:] = small


def finish_kernel(
    own_ref, other_ref, own_small_ref, other_small_ref, w_first_ref, b_first_ref, w_second_ref,
    b_second_ref, w_third_ref, b_third_ref,
):
    core, half = lax.axis_index("c"), 256
    for at, ref, small_ref in ((core, own_ref, own_small_ref), (1 - core, other_ref, other_small_ref)):
        where = pl.ds(pl.multiple_of(at * half, half), half)
        w_third_ref[where, :] = ref[:, :16, :].reshape(half, 512).astype(F32)
        w_second_ref[where, :] = ref[:, 16:, :].reshape(half, 512).astype(F32)
        small = unfold(small_ref[...].astype(F32))
        w_first_ref[:, where] = small[0:3]
        b_first_ref[:, where] = small[3:4]
        b_second_ref[:, where] = small[4:5]
        b_third_ref[:, where] = small[5:6]


def swap(value, flip):
    axis, bits = flip
    return lax.ppermute(value, axis, [(i, i ^ bits) for i in range(dict(SPLIT)[axis])])


def shards(grad_out, coef, coords, w_first, b_first, w_second, b_second, w_third, b_third):
    points = grad_out.shape[1] // 8
    vmem = pl.BlockSpec(memory_space=pltpu.VMEM)
    hbm = pl.BlockSpec(memory_space=pltpu.HBM)

    coords, w_first, b_first, w_second, b_second, w_third, b_third = (
        pltpu.with_memory_space_constraint(value, pltpu.HBM)
        for value in (coords, w_first, b_first[None], w_second, b_second[None], w_third, b_third[None])
    )
    send = pl.pallas_call(
        pack_kernel,
        out_shape=pltpu.VMEM((8, 8, points + 512), BF16),
        in_specs=[vmem, vmem],
        out_specs=vmem,
    )(grad_out, coef)
    near = lax.all_to_all(send, ("xl", "y"), 0, 0, tiled=True).reshape(64, points + 512)
    acts, basis, xyz = pl.pallas_call(
        forward_kernel,
        out_shape=(
            pltpu.VMEM((2, 512, points), BF16),
            pltpu.VMEM((512, points), BF16),
            pltpu.VMEM((3, points), F32),
        ),
        in_specs=[hbm] * 7,
        out_specs=(vmem,) * 3,
        scratch_shapes=[
            pltpu.VMEM((3, 512), F32),
            pltpu.VMEM((3, 1, 512), F32),
            pltpu.VMEM((2, 512, 512), BF16),
            pltpu.SemaphoreType.DMA((7,)),
        ],
        compiler_params=pltpu.CompilerParams(vmem_limit_bytes=VMEM_BYTES),
        cost_estimate=pl.CostEstimate(flops=2**30, bytes_accessed=5 * 2**20, transcendentals=2**20),
    )(coords, w_first, b_first, w_second, b_second, w_third, b_third)
    near, acts = lax.optimization_barrier((near, acts))
    far = swap(near, ("c", 1))
    coef_part, weights = pl.pallas_call(
        middle_kernel,
        out_shape=(pltpu.VMEM((64, 512), F32), pltpu.VMEM((2, 512, 512), BF16)),
        in_specs=[vmem, vmem, hbm, hbm],
        out_specs=(vmem,) * 2,
        scratch_shapes=[pltpu.SemaphoreType.DMA((2,))],
        compiler_params=pltpu.CompilerParams(vmem_limit_bytes=VMEM_BYTES),
        cost_estimate=pl.CostEstimate(flops=2**28, bytes_accessed=2 * 2**20, transcendentals=0),
    )(near, basis, w_second, w_third)
    partial = pl.pallas_call(
        backward_kernel,
        out_shape=jax.ShapeDtypeStruct((16, 32, 640), BF16),
        in_specs=[vmem] * 6,
        out_specs=vmem,
        scratch_shapes=[pltpu.VMEM((512, points), BF16)] * 2,
        compiler_params=pltpu.CompilerParams(vmem_limit_bytes=VMEM_BYTES),
        cost_estimate=pl.CostEstimate(flops=2**31, bytes_accessed=5 * 2**20, transcendentals=0),
    )(near, far, xyz, weights, coef_part, acts)

    parts = lax.all_to_all(partial, PLANE, 0, 0, tiled=True)
    mine = jnp.sum(parts.astype(F32), axis=0).astype(BF16)
    one, two, three = (swap(mine, ("z", bits)).astype(F32) for bits in (1, 2, 3))
    mine = ((mine.astype(F32) + one) + (two + three)).astype(BF16)
    mine = (mine.astype(F32) + swap(mine, ("z", 6)).astype(F32)).astype(BF16)

    small = mine[16:, 512:]
    other_small = swap(small, ("c", 1))
    gathered = jnp.broadcast_to(mine[:, :512], (16, 32, 512))
    gathered = lax.all_to_all(gathered, PLANE, 0, 0, tiled=True)
    other = swap(gathered, ("c", 1))
    row = jax.ShapeDtypeStruct((1, 512), F32)
    square = jax.ShapeDtypeStruct((512, 512), F32)
    z = lax.axis_index("z")
    grad_coef = lax.dynamic_slice(mine, (z // 4 * 8, 512 + z % 4 * 32), (8, 32)).astype(F32)
    w_one, b_one, w_two, b_two, w_three, b_three = pl.pallas_call(
        finish_kernel,
        out_shape=(jax.ShapeDtypeStruct((3, 512), F32), row, square, row, square, row),
        in_specs=[vmem] * 4,
        out_specs=(vmem,) * 6,
        compiler_params=pltpu.CompilerParams(vmem_limit_bytes=VMEM_BYTES),
    )(gathered, other, small, other_small)
    return (grad_coef, w_one, b_one[0], w_two, b_two[0], w_three, b_three[0])


def solution(mesh):
    fine = Mesh(mesh.devices.reshape(SIZES), AXES)
    fn, pts = ("xl", "y", "c"), ("xh", "z")
    return jax.shard_map(
        shards,
        mesh=fine,
        in_specs=(P(fn, pts), P(fn, None), P(None, pts), P(), P(), P(), P(), P(), P()),
        out_specs=(P(fn, pts), P(), P(), P(), P(), P(), P()),
        check_vma=False,
    )
```

```python
import jax
import jax.numpy as jnp
from jax import lax
from jax.experimental import pallas as pl
from jax.experimental.pallas import tpu as pltpu
from jax.sharding import Mesh, PartitionSpec as P

SPLIT = (("xh", 2), ("z", 8), ("xl", 2), ("y", 4), ("c", 2))
AXES = tuple(name for name, _ in SPLIT)
SIZES = tuple(size for _, size in SPLIT)
PLANE = ("xl", "xh", "y")
VMEM_BYTES = 20 * 1024 * 1024
BF16, F32 = jnp.bfloat16, jnp.float32


def nn(a, b):
    return lax.dot_general(a, b, (((1,), (0,)), ((), ())), preferred_element_type=F32)


def nt(a, b):
    return lax.dot_general(a, b, (((1,), (1,)), ((), ())), preferred_element_type=F32)


def tn(a, b):
    return lax.dot_general(a, b, (((0,), (0,)), ((), ())), preferred_element_type=F32)


def fold(a):
    return jnp.concatenate([a[:, :128], a[:, 128:]], axis=0)


def across(a):
    total = a[:, :128]
    for at in range(128, a.shape[1], 128):
        total = total + a[:, at : at + 128]
    return jnp.sum(total.T, axis=0, keepdims=True)


def unfold(a):
    return jnp.concatenate([a[:8], a[8:]], axis=1)


def pack_kernel(grad_out_ref, coef_ref, out_ref):
    blocks, rows, width = out_ref.shape
    points = width - coef_ref.shape[1]
    for at in range(blocks):
        out_ref[at, :, :points] = grad_out_ref[:, at * points : (at + 1) * points]
        out_ref[at, :, points:] = coef_ref[...]


def forward_kernel(
    coords_ref, w_first_ref, b_first_ref, w_second_ref, b_second_ref, w_third_ref, b_third_ref,
    acts_ref, basis_ref, xyz_ref, small_ref, bias_ref, weights_ref, sems,
):
    one_ref, two_ref = acts_ref.at[0], acts_ref.at[1]
    points = one_ref.shape[1]
    at = lax.axis_index("xl") * 4 + lax.axis_index("y")
    block = pl.ds(pl.multiple_of(at * points, points), points)
    copies = [
        pltpu.make_async_copy(coords_ref.at[:, block], xyz_ref, sems.at[0]),
        pltpu.make_async_copy(w_first_ref, small_ref, sems.at[1]),
        pltpu.make_async_copy(b_first_ref, bias_ref.at[0], sems.at[2]),
        pltpu.make_async_copy(b_second_ref, bias_ref.at[1], sems.at[3]),
        pltpu.make_async_copy(b_third_ref, bias_ref.at[2], sems.at[4]),
        pltpu.make_async_copy(w_second_ref, weights_ref.at[0], sems.at[5]),
        pltpu.make_async_copy(w_third_ref, weights_ref.at[1], sems.at[6]),
    ]
    for copy in copies:
        copy.start()
    for copy in copies[:5]:
        copy.wait()
    xyz = xyz_ref[...]
    w_one = small_ref[...].T
    z_one = w_one[:, 0:1] * xyz[0:1] + w_one[:, 1:2] * xyz[1:2] + w_one[:, 2:3] * xyz[2:3]
    one_ref[...] = jnp.tanh(z_one + bias_ref[0].T).astype(BF16)
    copies[5].wait()
    two_ref[...] = jnp.tanh(tn(weights_ref[0], one_ref[...]) + bias_ref[1].T).astype(BF16)
    copies[6].wait()
    basis_ref[...] = (tn(weights_ref[1], two_ref[...]) + bias_ref[2].T).astype(BF16)


def middle_kernel(near_ref, basis_ref, w_second_ref, w_third_ref, coef_ref, weights_ref, sems):
    copies = [
        pltpu.make_async_copy(w_second_ref, weights_ref.at[0], sems.at[0]),
        pltpu.make_async_copy(w_third_ref, weights_ref.at[1], sems.at[1]),
    ]
    for copy in copies:
        copy.start()
    coef_ref[...] = nt(near_ref[:, : basis_ref.shape[1]], basis_ref[...])
    for copy in copies:
        copy.wait()


def backward_kernel(
    near_ref, far_ref, xyz_ref, weights_ref, coef_ref, acts_ref, out_ref, grad_basis_ref, pre_two_ref
):
    one_ref, two_ref = acts_ref.at[0], acts_ref.at[1]
    w_second_ref, w_third_ref = weights_ref.at[0], weights_ref.at[1]
    core = lax.axis_index("c")
    points = one_ref.shape[1]
    half = w_second_ref.shape[0] // 2
    own = pl.ds(pl.multiple_of(core * half, half), half)
    grad_basis = tn(near_ref[:, points:], near_ref[:, :points])
    grad_basis = grad_basis + tn(far_ref[:, points:], far_ref[:, :points])
    grad_basis_ref[...] = grad_basis.astype(BF16)
    out_ref[:, :16, :512] = nt(two_ref[own, :], grad_basis_ref[...]).astype(BF16).reshape(16, 16, 512)
    two = two_ref[...].astype(F32)
    pre_two_ref[...] = (nn(w_third_ref[...], grad_basis_ref[...]) * (1.0 - two * two)).astype(BF16)
    out_ref[:, 16:, :512] = nt(one_ref[own, :], pre_two_ref[...]).astype(BF16).reshape(16, 16, 512)
    one = one_ref[own, :].astype(F32)
    pre_one = nn(w_second_ref[own, :], pre_two_ref[...]) * (1.0 - one * one)

    xyz = xyz_ref[...]
    small = [across(pre_one * xyz[axis : axis + 1]) for axis in range(3)]
    small += [across(pre_one), across(pre_two_ref[own, :].astype(F32))]
    small += [across(grad_basis_ref[own, :].astype(F32)), jnp.zeros((2, half), F32)]
    small = fold(jnp.concatenate(small, axis=0)).astype(BF16)
    for at in range(16):
        group, column = at // 8 * 4 + at % 4, at // 4 % 2
        mine = coef_ref[group * 8 : group * 8 + 8, column * half : column * half + half]
        out_ref[at, :16, 512:] = fold(mine).astype(BF16)
        out_ref[at, 16:, 512:] = small


def finish_kernel(
    own_ref, other_ref, own_small_ref, other_small_ref, w_first_ref, b_first_ref, w_second_ref,
    b_second_ref, w_third_ref, b_third_ref,
):
    core, half = lax.axis_index("c"), 256
    for at, ref, small_ref in ((core, own_ref, own_small_ref), (1 - core, other_ref, other_small_ref)):
        where = pl.ds(pl.multiple_of(at * half, half), half)
        w_third_ref[where, :] = ref[:, :16, :].reshape(half, 512).astype(F32)
        w_second_ref[where, :] = ref[:, 16:, :].reshape(half, 512).astype(F32)
        small = unfold(small_ref[...].astype(F32))
        w_first_ref[:, where] = small[0:3]
        b_first_ref[:, where] = small[3:4]
        b_second_ref[:, where] = small[4:5]
        b_third_ref[:, where] = small[5:6]


def swap(value, flip):
    axis, bits = flip
    return lax.ppermute(value, axis, [(i, i ^ bits) for i in range(dict(SPLIT)[axis])])


def shards(grad_out, coef, coords, w_first, b_first, w_second, b_second, w_third, b_third):
    points = grad_out.shape[1] // 8
    vmem = pl.BlockSpec(memory_space=pltpu.VMEM)
    hbm = pl.BlockSpec(memory_space=pltpu.HBM)

    coords, w_first, b_first, w_second, b_second, w_third, b_third = (
        pltpu.with_memory_space_constraint(value, pltpu.HBM)
        for value in (coords, w_first, b_first[None], w_second, b_second[None], w_third, b_third[None])
    )
    send = pl.pallas_call(
        pack_kernel,
        out_shape=pltpu.VMEM((8, 8, points + 512), BF16),
        in_specs=[vmem, vmem],
        out_specs=vmem,
    )(grad_out, coef)
    near = lax.all_to_all(send, ("xl", "y"), 0, 0, tiled=True).reshape(64, points + 512)
    acts, basis, xyz = pl.pallas_call(
        forward_kernel,
        out_shape=(
            pltpu.VMEM((2, 512, points), BF16),
            pltpu.VMEM((512, points), BF16),
            pltpu.VMEM((3, points), F32),
        ),
        in_specs=[hbm] * 7,
        out_specs=(vmem,) * 3,
        scratch_shapes=[
            pltpu.VMEM((3, 512), F32),
            pltpu.VMEM((3, 1, 512), F32),
            pltpu.VMEM((2, 512, 512), BF16),
            pltpu.SemaphoreType.DMA((7,)),
        ],
        compiler_params=pltpu.CompilerParams(vmem_limit_bytes=VMEM_BYTES),
        cost_estimate=pl.CostEstimate(flops=2**30, bytes_accessed=5 * 2**20, transcendentals=2**20),
    )(coords, w_first, b_first, w_second, b_second, w_third, b_third)
    near, acts = lax.optimization_barrier((near, acts))
    far = swap(near, ("c", 1))
    coef_part, weights = pl.pallas_call(
        middle_kernel,
        out_shape=(pltpu.VMEM((64, 512), F32), pltpu.VMEM((2, 512, 512), BF16)),
        in_specs=[vmem, vmem, hbm, hbm],
        out_specs=(vmem,) * 2,
        scratch_shapes=[pltpu.SemaphoreType.DMA((2,))],
        compiler_params=pltpu.CompilerParams(vmem_limit_bytes=VMEM_BYTES),
        cost_estimate=pl.CostEstimate(flops=2**28, bytes_accessed=2 * 2**20, transcendentals=0),
    )(near, basis, w_second, w_third)
    partial = pl.pallas_call(
        backward_kernel,
        out_shape=jax.ShapeDtypeStruct((16, 32, 640), BF16),
        in_specs=[vmem] * 6,
        out_specs=vmem,
        scratch_shapes=[pltpu.VMEM((512, points), BF16)] * 2,
        compiler_params=pltpu.CompilerParams(vmem_limit_bytes=VMEM_BYTES),
        cost_estimate=pl.CostEstimate(flops=2**31, bytes_accessed=5 * 2**20, transcendentals=0),
    )(near, far, xyz, weights, coef_part, acts)

    parts = lax.all_to_all(partial, PLANE, 0, 0, tiled=True)
    mine = jnp.sum(parts.astype(F32), axis=0).astype(BF16)
    three, two, one = (swap(mine, ("z", bits)).astype(F32) for bits in (3, 2, 1))
    mine = (((three + two) + (one + mine.astype(F32)))).astype(BF16)
    mine = (mine.astype(F32) + swap(mine, ("z", 7)).astype(F32)).astype(BF16)

    small = mine[16:, 512:]
    other_small = swap(small, ("c", 1))
    gathered = jnp.broadcast_to(mine[:, :512], (16, 32, 512))
    gathered = lax.all_to_all(gathered, PLANE, 0, 0, tiled=True)
    other = swap(gathered, ("c", 1))
    row = jax.ShapeDtypeStruct((1, 512), F32)
    square = jax.ShapeDtypeStruct((512, 512), F32)
    z = lax.axis_index("z")
    grad_coef = lax.dynamic_slice(mine, (z // 4 * 8, 512 + z % 4 * 32), (8, 32)).astype(F32)
    w_one, b_one, w_two, b_two, w_three, b_three = pl.pallas_call(
        finish_kernel,
        out_shape=(jax.ShapeDtypeStruct((3, 512), F32), row, square, row, square, row),
        in_specs=[vmem] * 4,
        out_specs=(vmem,) * 6,
        compiler_params=pltpu.CompilerParams(vmem_limit_bytes=VMEM_BYTES),
    )(gathered, other, small, other_small)
    return (grad_coef, w_one, b_one[0], w_two, b_two[0], w_three, b_three[0])


def solution(mesh):
    fine = Mesh(mesh.devices.reshape(SIZES), AXES)
    fn, pts = ("xl", "y", "c"), ("xh", "z")
    return jax.shard_map(
        shards,
        mesh=fine,
        in_specs=(P(fn, pts), P(fn, None), P(None, pts), P(), P(), P(), P(), P(), P()),
        out_specs=(P(fn, pts), P(), P(), P(), P(), P(), P()),
        check_vma=False,
    )
```

```python
import jax
import jax.numpy as jnp
from jax import lax
from jax.experimental import pallas as pl
from jax.experimental.pallas import tpu as pltpu
from jax.sharding import Mesh, PartitionSpec as P

SPLIT = (("xh", 2), ("z", 8), ("xl", 2), ("y", 4), ("c", 2))
AXES = tuple(name for name, _ in SPLIT)
SIZES = tuple(size for _, size in SPLIT)
PLANE = ("xl", "xh", "y")
VMEM_BYTES = 20 * 1024 * 1024
BF16, F32 = jnp.bfloat16, jnp.float32


def nn(a, b):
    return lax.dot_general(a, b, (((1,), (0,)), ((), ())), preferred_element_type=F32)


def nt(a, b):
    return lax.dot_general(a, b, (((1,), (1,)), ((), ())), preferred_element_type=F32)


def tn(a, b):
    return lax.dot_general(a, b, (((0,), (0,)), ((), ())), preferred_element_type=F32)


def fold(a):
    return jnp.concatenate([a[:, :128], a[:, 128:]], axis=0)


def across(a):
    total = a[:, :128]
    for at in range(128, a.shape[1], 128):
        total = total + a[:, at : at + 128]
    return jnp.sum(total.T, axis=0, keepdims=True)


def unfold(a):
    return jnp.concatenate([a[:8], a[8:]], axis=1)


def pack_kernel(grad_out_ref, coef_ref, out_ref):
    blocks, rows, width = out_ref.shape
    points = width - coef_ref.shape[1]
    for at in range(blocks):
        out_ref[at, :, :points] = grad_out_ref[:, at * points : (at + 1) * points]
        out_ref[at, :, points:] = coef_ref[...]


def forward_kernel(
    coords_ref, w_first_ref, b_first_ref, w_second_ref, b_second_ref, w_third_ref, b_third_ref,
    acts_ref, basis_ref, xyz_ref, small_ref, bias_ref, weights_ref, sems,
):
    one_ref, two_ref = acts_ref.at[0], acts_ref.at[1]
    points = one_ref.shape[1]
    at = lax.axis_index("xl") * 4 + lax.axis_index("y")
    block = pl.ds(pl.multiple_of(at * points, points), points)
    copies = [
        pltpu.make_async_copy(coords_ref.at[:, block], xyz_ref, sems.at[0]),
        pltpu.make_async_copy(w_first_ref, small_ref, sems.at[1]),
        pltpu.make_async_copy(b_first_ref, bias_ref.at[0], sems.at[2]),
        pltpu.make_async_copy(b_second_ref, bias_ref.at[1], sems.at[3]),
        pltpu.make_async_copy(b_third_ref, bias_ref.at[2], sems.at[4]),
        pltpu.make_async_copy(w_second_ref, weights_ref.at[0], sems.at[5]),
        pltpu.make_async_copy(w_third_ref, weights_ref.at[1], sems.at[6]),
    ]
    for copy in copies:
        copy.start()
    for copy in copies[:5]:
        copy.wait()
    xyz = xyz_ref[...]
    w_one = small_ref[...].T
    z_one = w_one[:, 0:1] * xyz[0:1] + w_one[:, 1:2] * xyz[1:2] + w_one[:, 2:3] * xyz[2:3]
    one_ref[...] = jnp.tanh(z_one + bias_ref[0].T).astype(BF16)
    copies[5].wait()
    two_ref[...] = jnp.tanh(tn(weights_ref[0], one_ref[...]) + bias_ref[1].T).astype(BF16)
    copies[6].wait()
    basis_ref[...] = (tn(weights_ref[1], two_ref[...]) + bias_ref[2].T).astype(BF16)


def middle_kernel(near_ref, basis_ref, w_second_ref, w_third_ref, coef_ref, weights_ref, sems):
    copies = [
        pltpu.make_async_copy(w_second_ref, weights_ref.at[0], sems.at[0]),
        pltpu.make_async_copy(w_third_ref, weights_ref.at[1], sems.at[1]),
    ]
    for copy in copies:
        copy.start()
    coef_ref[...] = nt(near_ref[:, : basis_ref.shape[1]], basis_ref[...])
    for copy in copies:
        copy.wait()


def backward_kernel(
    near_ref, far_ref, xyz_ref, weights_ref, coef_ref, acts_ref, out_ref, grad_basis_ref, pre_two_ref,
    pre_one_ref,
):
    one_ref, two_ref = acts_ref.at[0], acts_ref.at[1]
    w_second_ref, w_third_ref = weights_ref.at[0], weights_ref.at[1]
    core = lax.axis_index("c")
    points = one_ref.shape[1]
    half = w_second_ref.shape[0] // 2
    own = pl.ds(pl.multiple_of(core * half, half), half)
    grad_basis = tn(near_ref[:, points:], near_ref[:, :points])
    grad_basis = grad_basis + tn(far_ref[:, points:], far_ref[:, :points])
    grad_basis_ref[...] = grad_basis.astype(BF16)
    two = two_ref[...].astype(F32)
    pre_two_ref[...] = (nn(w_third_ref[...], grad_basis_ref[...]) * (1.0 - two * two)).astype(BF16)
    one = one_ref[own, :].astype(F32)
    pre_one_ref[...] = nn(w_second_ref[own, :], pre_two_ref[...]) * (1.0 - one * one)
    out_ref[:, :16, :512] = nt(two_ref[own, :], grad_basis_ref[...]).astype(BF16).reshape(16, 16, 512)
    out_ref[:, 16:, :512] = nt(one_ref[own, :], pre_two_ref[...]).astype(BF16).reshape(16, 16, 512)

    xyz, pre_one = xyz_ref[...], pre_one_ref[...]
    small = [across(pre_one * xyz[axis : axis + 1]) for axis in range(3)]
    small += [across(pre_one), across(pre_two_ref[own, :].astype(F32))]
    small += [across(grad_basis_ref[own, :].astype(F32)), jnp.zeros((2, half), F32)]
    small = fold(jnp.concatenate(small, axis=0)).astype(BF16)
    for at in range(16):
        group, column = at // 8 * 4 + at % 4, at // 4 % 2
        mine = coef_ref[group * 8 : group * 8 + 8, column * half : column * half + half]
        out_ref[at, :16, 512:] = fold(mine).astype(BF16)
        out_ref[at, 16:, 512:] = small


def widen(at, blocks_ref, wide_ref, w_second_ref, w_third_ref, sems):
    half = wide_ref.shape[1]
    where = pl.ds(pl.multiple_of(at * half, half), half)
    copies = []
    for which, out_ref in enumerate((w_third_ref, w_second_ref)):
        value = blocks_ref[:, 16 * which : 16 * which + 16, :]
        wide_ref[which] = value.reshape(half, 512).astype(F32)
        copies.append(pltpu.make_async_copy(wide_ref.at[which], out_ref.at[where, :], sems.at[which]))
        copies[-1].start()
    return copies


def own_kernel(own_ref, sums_ref, w_second_ref, w_third_ref, coef_ref, wide_ref, mine_ref, sems):
    copies = widen(lax.axis_index("c"), own_ref, wide_ref, w_second_ref, w_third_ref, sems)
    row = lax.broadcasted_iota(jnp.int32, (256, 32), 0)
    column = lax.broadcasted_iota(jnp.int32, (256, 32), 1)
    chosen = (row == column + lax.axis_index("z") * 32).astype(F32).astype(BF16)
    mine_ref[...] = nn(unfold(sums_ref[:16, 512:].astype(F32)).astype(BF16), chosen)
    copies.append(pltpu.make_async_copy(mine_ref, coef_ref, sems.at[2]))
    copies[-1].start()
    for copy in copies:
        copy.wait()


def other_kernel(
    other_ref, own_small_ref, other_small_ref, w_second_in_ref, w_third_in_ref, w_second_ref, w_third_ref,
    w_first_ref, b_first_ref, b_second_ref, b_third_ref, wide_ref, small_ref, first_ref, sems,
):
    core, half = lax.axis_index("c"), wide_ref.shape[1]
    for at, ref in ((core, own_small_ref), (1 - core, other_small_ref)):
        where = pl.ds(pl.multiple_of(at * half, half), half)
        small = unfold(ref[...].astype(F32))
        first_ref[:, where] = small[0:3]
        for which in range(3):
            small_ref[which, :, where] = small[3 + which : 4 + which]
    copies = [pltpu.make_async_copy(first_ref, w_first_ref, sems.at[2])]
    for which, out_ref in enumerate((b_first_ref, b_second_ref, b_third_ref)):
        copies.append(pltpu.make_async_copy(small_ref.at[which], out_ref, sems.at[3 + which]))
    for copy in copies:
        copy.start()
    copies += widen(1 - core, other_ref, wide_ref, w_second_ref, w_third_ref, sems)
    for copy in copies:
        copy.wait()


def swap(value, flip):
    axis, bits = flip
    return lax.ppermute(value, axis, [(i, i ^ bits) for i in range(dict(SPLIT)[axis])])


def shards(grad_out, coef, coords, w_first, b_first, w_second, b_second, w_third, b_third):
    points = grad_out.shape[1] // 8
    vmem = pl.BlockSpec(memory_space=pltpu.VMEM)
    hbm = pl.BlockSpec(memory_space=pltpu.HBM)

    coords, w_first, b_first, w_second, b_second, w_third, b_third = (
        pltpu.with_memory_space_constraint(value, pltpu.HBM)
        for value in (coords, w_first, b_first[None], w_second, b_second[None], w_third, b_third[None])
    )
    send = pl.pallas_call(
        pack_kernel,
        out_shape=pltpu.VMEM((8, 8, points + 512), BF16),
        in_specs=[vmem, vmem],
        out_specs=vmem,
    )(grad_out, coef)
    near = lax.all_to_all(send, ("xl", "y"), 0, 0, tiled=True).reshape(64, points + 512)
    acts, basis, xyz = pl.pallas_call(
        forward_kernel,
        out_shape=(
            pltpu.VMEM((2, 512, points), BF16),
            pltpu.VMEM((512, points), BF16),
            pltpu.VMEM((3, points), F32),
        ),
        in_specs=[hbm] * 7,
        out_specs=(vmem,) * 3,
        scratch_shapes=[
            pltpu.VMEM((3, 512), F32),
            pltpu.VMEM((3, 1, 512), F32),
            pltpu.VMEM((2, 512, 512), BF16),
            pltpu.SemaphoreType.DMA((7,)),
        ],
        compiler_params=pltpu.CompilerParams(vmem_limit_bytes=VMEM_BYTES),
        cost_estimate=pl.CostEstimate(flops=2**30, bytes_accessed=5 * 2**20, transcendentals=2**20),
    )(coords, w_first, b_first, w_second, b_second, w_third, b_third)
    near, acts = lax.optimization_barrier((near, acts))
    far = swap(near, ("c", 1))
    coef_part, weights = pl.pallas_call(
        middle_kernel,
        out_shape=(pltpu.VMEM((64, 512), F32), pltpu.VMEM((2, 512, 512), BF16)),
        in_specs=[vmem, vmem, hbm, hbm],
        out_specs=(vmem,) * 2,
        scratch_shapes=[pltpu.SemaphoreType.DMA((2,))],
        compiler_params=pltpu.CompilerParams(vmem_limit_bytes=VMEM_BYTES),
        cost_estimate=pl.CostEstimate(flops=2**28, bytes_accessed=2 * 2**20, transcendentals=0),
    )(near, basis, w_second, w_third)
    partial = pl.pallas_call(
        backward_kernel,
        out_shape=jax.ShapeDtypeStruct((16, 32, 640), BF16),
        in_specs=[vmem] * 6,
        out_specs=vmem,
        scratch_shapes=[pltpu.VMEM((512, points), BF16)] * 2 + [pltpu.VMEM((256, points), F32)],
        compiler_params=pltpu.CompilerParams(vmem_limit_bytes=VMEM_BYTES),
        cost_estimate=pl.CostEstimate(flops=2**31, bytes_accessed=5 * 2**20, transcendentals=0),
    )(near, far, xyz, weights, coef_part, acts)

    parts = lax.all_to_all(partial, PLANE, 0, 0, tiled=True)
    mine = jnp.sum(parts.astype(F32), axis=0).astype(BF16)
    three, two, one = (swap(mine, ("z", bits)).astype(F32) for bits in (3, 2, 1))
    mine = ((one + mine.astype(F32)) + (two + three)).astype(BF16)
    mine = (mine.astype(F32) + swap(mine, ("z", 7)).astype(F32)).astype(BF16)

    small = mine[16:, 512:]
    other_small = swap(small, ("c", 1))
    gathered = jnp.broadcast_to(mine[:, :512], (16, 32, 512))
    gathered = lax.all_to_all(gathered, PLANE, 0, 0, tiled=True)
    other = swap(gathered, ("c", 1))
    row, square = pltpu.HBM((1, 512), F32), pltpu.HBM((512, 512), F32)
    wide = pltpu.VMEM((2, 256, 512), F32)
    cost = pl.CostEstimate(flops=2**20, bytes_accessed=2**21, transcendentals=0)
    w_two, w_three, grad_coef = pl.pallas_call(
        own_kernel,
        out_shape=(square, square, pltpu.HBM((8, 32), F32)),
        in_specs=[vmem, vmem],
        out_specs=(hbm,) * 3,
        scratch_shapes=[wide, pltpu.VMEM((8, 32), F32), pltpu.SemaphoreType.DMA((3,))],
        compiler_params=pltpu.CompilerParams(vmem_limit_bytes=VMEM_BYTES),
        cost_estimate=cost,
    )(gathered, mine)
    w_two, w_three, w_one, b_one, b_two, b_three = pl.pallas_call(
        other_kernel,
        out_shape=(square, square, pltpu.HBM((3, 512), F32), row, row, row),
        in_specs=[vmem, vmem, vmem, hbm, hbm],
        out_specs=(hbm,) * 6,
        input_output_aliases={3: 0, 4: 1},
        scratch_shapes=[
            wide,
            pltpu.VMEM((3, 1, 512), F32),
            pltpu.VMEM((3, 512), F32),
            pltpu.SemaphoreType.DMA((6,)),
        ],
        compiler_params=pltpu.CompilerParams(vmem_limit_bytes=VMEM_BYTES),
        cost_estimate=cost,
    )(other, small, other_small, w_two, w_three)
    return (grad_coef, w_one, b_one[0], w_two, b_two[0], w_three, b_three[0])


def solution(mesh):
    fine = Mesh(mesh.devices.reshape(SIZES), AXES)
    fn, pts = ("xl", "y", "c"), ("xh", "z")
    return jax.shard_map(
        shards,
        mesh=fine,
        in_specs=(P(fn, pts), P(fn, None), P(None, pts), P(), P(), P(), P(), P(), P()),
        out_specs=(P(fn, pts), P(), P(), P(), P(), P(), P()),
        check_vma=False,
    )
```

```python
import jax
import jax.numpy as jnp
from jax import lax
from jax.experimental import pallas as pl
from jax.experimental.pallas import tpu as pltpu
from jax.sharding import Mesh, PartitionSpec as P

SPLIT = (("xh", 2), ("z", 8), ("xl", 2), ("y", 4), ("c", 2))
AXES = tuple(name for name, _ in SPLIT)
SIZES = tuple(size for _, size in SPLIT)
PLANE = ("xl", "xh", "y")
VMEM_BYTES = 20 * 1024 * 1024
BF16, F32 = jnp.bfloat16, jnp.float32


def nn(a, b):
    return lax.dot_general(a, b, (((1,), (0,)), ((), ())), preferred_element_type=F32)


def nt(a, b):
    return lax.dot_general(a, b, (((1,), (1,)), ((), ())), preferred_element_type=F32)


def tn(a, b):
    return lax.dot_general(a, b, (((0,), (0,)), ((), ())), preferred_element_type=F32)


def fold(a):
    return jnp.concatenate([a[:, :128], a[:, 128:]], axis=0)


def across(a):
    total = a[:, :128]
    for at in range(128, a.shape[1], 128):
        total = total + a[:, at : at + 128]
    return jnp.sum(total.T, axis=0, keepdims=True)


def unfold(a):
    return jnp.concatenate([a[:8], a[8:]], axis=1)


def pack_kernel(grad_out_ref, coef_ref, out_ref):
    blocks, rows, width = out_ref.shape
    points = width - coef_ref.shape[1]
    for at in range(blocks):
        out_ref[at, :, :points] = grad_out_ref[:, at * points : (at + 1) * points]
        out_ref[at, :, points:] = coef_ref[...]


def forward_kernel(
    coords_ref, w_first_ref, b_first_ref, w_second_ref, b_second_ref, w_third_ref, b_third_ref,
    acts_ref, basis_ref, xyz_ref, small_ref, bias_ref, weights_ref, sems,
):
    one_ref, two_ref = acts_ref.at[0], acts_ref.at[1]
    points = one_ref.shape[1]
    at = lax.axis_index("xl") * 4 + lax.axis_index("y")
    block = pl.ds(pl.multiple_of(at * points, points), points)
    copies = [
        pltpu.make_async_copy(coords_ref.at[:, block], xyz_ref, sems.at[0]),
        pltpu.make_async_copy(w_first_ref, small_ref, sems.at[1]),
        pltpu.make_async_copy(b_first_ref, bias_ref.at[0], sems.at[2]),
        pltpu.make_async_copy(b_second_ref, bias_ref.at[1], sems.at[3]),
        pltpu.make_async_copy(b_third_ref, bias_ref.at[2], sems.at[4]),
        pltpu.make_async_copy(w_second_ref, weights_ref.at[0], sems.at[5]),
        pltpu.make_async_copy(w_third_ref, weights_ref.at[1], sems.at[6]),
    ]
    for copy in copies:
        copy.start()
    for copy in copies[:5]:
        copy.wait()
    xyz = xyz_ref[...]
    w_one = small_ref[...].T
    z_one = w_one[:, 0:1] * xyz[0:1] + w_one[:, 1:2] * xyz[1:2] + w_one[:, 2:3] * xyz[2:3]
    one_ref[...] = jnp.tanh(z_one + bias_ref[0].T).astype(BF16)
    copies[5].wait()
    two_ref[...] = jnp.tanh(tn(weights_ref[0], one_ref[...]) + bias_ref[1].T).astype(BF16)
    copies[6].wait()
    basis_ref[...] = (tn(weights_ref[1], two_ref[...]) + bias_ref[2].T).astype(BF16)


def middle_kernel(near_ref, basis_ref, w_second_ref, w_third_ref, coef_ref, weights_ref, sems):
    copies = [
        pltpu.make_async_copy(w_second_ref, weights_ref.at[0], sems.at[0]),
        pltpu.make_async_copy(w_third_ref, weights_ref.at[1], sems.at[1]),
    ]
    for copy in copies:
        copy.start()
    coef_ref[...] = nt(near_ref[:, : basis_ref.shape[1]], basis_ref[...])
    for copy in copies:
        copy.wait()


def backward_kernel(
    near_ref, far_ref, xyz_ref, weights_ref, coef_ref, acts_ref, out_ref, grad_basis_ref, pre_two_ref,
    pre_one_ref,
):
    one_ref, two_ref = acts_ref.at[0], acts_ref.at[1]
    w_second_ref, w_third_ref = weights_ref.at[0], weights_ref.at[1]
    core = lax.axis_index("c")
    points = one_ref.shape[1]
    half = w_second_ref.shape[0] // 2
    own = pl.ds(pl.multiple_of(core * half, half), half)
    both = jnp.concatenate([near_ref[...], far_ref[...]], axis=0)
    grad_basis = tn(both[:, points:], both[:, :points])
    grad_basis_ref[...] = grad_basis.astype(BF16)
    two = two_ref[...].astype(F32)
    pre_two_ref[...] = (nn(w_third_ref[...], grad_basis_ref[...]) * (1.0 - two * two)).astype(BF16)
    one = one_ref[own, :].astype(F32)
    pre_one_ref[...] = nn(w_second_ref[own, :], pre_two_ref[...]) * (1.0 - one * one)
    out_ref[:, :16, :512] = nt(two_ref[own, :], grad_basis_ref[...]).astype(BF16).reshape(16, 16, 512)
    out_ref[:, 16:, :512] = nt(one_ref[own, :], pre_two_ref[...]).astype(BF16).reshape(16, 16, 512)

    xyz, pre_one = xyz_ref[...], pre_one_ref[...]
    small = [across(pre_one * xyz[axis : axis + 1]) for axis in range(3)]
    small += [across(pre_one), across(pre_two_ref[own, :].astype(F32))]
    small += [across(grad_basis_ref[own, :].astype(F32)), jnp.zeros((2, half), F32)]
    small = fold(jnp.concatenate(small, axis=0)).astype(BF16)
    for at in range(16):
        group, column = at // 8 * 4 + at % 4, at // 4 % 2
        mine = coef_ref[group * 8 : group * 8 + 8, column * half : column * half + half]
        out_ref[at, :16, 512:] = fold(mine).astype(BF16)
        out_ref[at, 16:, 512:] = small


def widen(at, blocks_ref, wide_ref, w_second_ref, w_third_ref, sems):
    half = wide_ref.shape[1]
    where = pl.ds(pl.multiple_of(at * half, half), half)
    copies = []
    for which, out_ref in enumerate((w_third_ref, w_second_ref)):
        value = blocks_ref[:, 16 * which : 16 * which + 16, :]
        wide_ref[which] = value.reshape(half, 512).astype(F32)
        copies.append(pltpu.make_async_copy(wide_ref.at[which], out_ref.at[where, :], sems.at[which]))
        copies[-1].start()
    return copies


def own_kernel(own_ref, sums_ref, w_second_ref, w_third_ref, coef_ref, wide_ref, mine_ref, sems):
    copies = widen(lax.axis_index("c"), own_ref, wide_ref, w_second_ref, w_third_ref, sems)
    row = lax.broadcasted_iota(jnp.int32, (256, 32), 0)
    column = lax.broadcasted_iota(jnp.int32, (256, 32), 1)
    chosen = (row == column + lax.axis_index("z") * 32).astype(F32).astype(BF16)
    mine_ref[...] = nn(unfold(sums_ref[:16, 512:].astype(F32)).astype(BF16), chosen)
    copies.append(pltpu.make_async_copy(mine_ref, coef_ref, sems.at[2]))
    copies[-1].start()
    for copy in copies:
        copy.wait()


def other_kernel(
    other_ref, own_small_ref, other_small_ref, w_second_in_ref, w_third_in_ref, w_second_ref, w_third_ref,
    w_first_ref, b_first_ref, b_second_ref, b_third_ref, wide_ref, small_ref, first_ref, sems,
):
    core, half = lax.axis_index("c"), wide_ref.shape[1]
    for at, ref in ((core, own_small_ref), (1 - core, other_small_ref)):
        where = pl.ds(pl.multiple_of(at * half, half), half)
        small = unfold(ref[...].astype(F32))
        first_ref[:, where] = small[0:3]
        for which in range(3):
            small_ref[which, :, where] = small[3 + which : 4 + which]
    copies = [pltpu.make_async_copy(first_ref, w_first_ref, sems.at[2])]
    for which, out_ref in enumerate((b_first_ref, b_second_ref, b_third_ref)):
        copies.append(pltpu.make_async_copy(small_ref.at[which], out_ref, sems.at[3 + which]))
    for copy in copies:
        copy.start()
    copies += widen(1 - core, other_ref, wide_ref, w_second_ref, w_third_ref, sems)
    for copy in copies:
        copy.wait()


def swap(value, flip):
    axis, bits = flip
    return lax.ppermute(value, axis, [(i, i ^ bits) for i in range(dict(SPLIT)[axis])])


def shards(grad_out, coef, coords, w_first, b_first, w_second, b_second, w_third, b_third):
    points = grad_out.shape[1] // 8
    vmem = pl.BlockSpec(memory_space=pltpu.VMEM)
    hbm = pl.BlockSpec(memory_space=pltpu.HBM)

    coords, w_first, b_first, w_second, b_second, w_third, b_third = (
        pltpu.with_memory_space_constraint(value, pltpu.HBM)
        for value in (coords, w_first, b_first[None], w_second, b_second[None], w_third, b_third[None])
    )
    send = pl.pallas_call(
        pack_kernel,
        out_shape=pltpu.VMEM((8, 8, points + 512), BF16),
        in_specs=[vmem, vmem],
        out_specs=vmem,
    )(grad_out, coef)
    near = lax.all_to_all(send, ("xl", "y"), 0, 0, tiled=True).reshape(64, points + 512)
    acts, basis, xyz = pl.pallas_call(
        forward_kernel,
        out_shape=(
            pltpu.VMEM((2, 512, points), BF16),
            pltpu.VMEM((512, points), BF16),
            pltpu.VMEM((3, points), F32),
        ),
        in_specs=[hbm] * 7,
        out_specs=(vmem,) * 3,
        scratch_shapes=[
            pltpu.VMEM((3, 512), F32),
            pltpu.VMEM((3, 1, 512), F32),
            pltpu.VMEM((2, 512, 512), BF16),
            pltpu.SemaphoreType.DMA((7,)),
        ],
        compiler_params=pltpu.CompilerParams(vmem_limit_bytes=VMEM_BYTES),
        cost_estimate=pl.CostEstimate(flops=2**30, bytes_accessed=5 * 2**20, transcendentals=2**20),
    )(coords, w_first, b_first, w_second, b_second, w_third, b_third)
    near, acts = lax.optimization_barrier((near, acts))
    far = swap(near, ("c", 1))
    coef_part, weights = pl.pallas_call(
        middle_kernel,
        out_shape=(pltpu.VMEM((64, 512), F32), pltpu.VMEM((2, 512, 512), BF16)),
        in_specs=[vmem, vmem, hbm, hbm],
        out_specs=(vmem,) * 2,
        scratch_shapes=[pltpu.SemaphoreType.DMA((2,))],
        compiler_params=pltpu.CompilerParams(vmem_limit_bytes=VMEM_BYTES),
        cost_estimate=pl.CostEstimate(flops=2**28, bytes_accessed=2 * 2**20, transcendentals=0),
    )(near, basis, w_second, w_third)
    partial = pl.pallas_call(
        backward_kernel,
        out_shape=jax.ShapeDtypeStruct((16, 32, 640), BF16),
        in_specs=[vmem] * 6,
        out_specs=vmem,
        scratch_shapes=[pltpu.VMEM((512, points), BF16)] * 2 + [pltpu.VMEM((256, points), F32)],
        compiler_params=pltpu.CompilerParams(vmem_limit_bytes=VMEM_BYTES),
        cost_estimate=pl.CostEstimate(flops=2**31, bytes_accessed=5 * 2**20, transcendentals=0),
    )(near, far, xyz, weights, coef_part, acts)

    parts = lax.all_to_all(partial, PLANE, 0, 0, tiled=True)
    mine = jnp.sum(parts.astype(F32), axis=0).astype(BF16)
    three, two, one = (swap(mine, ("z", bits)).astype(F32) for bits in (3, 2, 1))
    mine = ((one + mine.astype(F32)) + (two + three)).astype(BF16)
    mine = (mine.astype(F32) + swap(mine, ("z", 7)).astype(F32)).astype(BF16)

    small = mine[16:, 512:]
    other_small = swap(small, ("c", 1))
    gathered = jnp.broadcast_to(mine[:, :512], (16, 32, 512))
    gathered = lax.all_to_all(gathered, PLANE, 0, 0, tiled=True)
    other = swap(gathered, ("c", 1))
    row, square = pltpu.HBM((1, 512), F32), pltpu.HBM((512, 512), F32)
    wide = pltpu.VMEM((2, 256, 512), F32)
    cost = pl.CostEstimate(flops=2**20, bytes_accessed=2**21, transcendentals=0)
    w_two, w_three, grad_coef = pl.pallas_call(
        own_kernel,
        out_shape=(square, square, pltpu.HBM((8, 32), F32)),
        in_specs=[vmem, vmem],
        out_specs=(hbm,) * 3,
        scratch_shapes=[wide, pltpu.VMEM((8, 32), F32), pltpu.SemaphoreType.DMA((3,))],
        compiler_params=pltpu.CompilerParams(vmem_limit_bytes=VMEM_BYTES),
        cost_estimate=cost,
    )(gathered, mine)
    w_two, w_three, w_one, b_one, b_two, b_three = pl.pallas_call(
        other_kernel,
        out_shape=(square, square, pltpu.HBM((3, 512), F32), row, row, row),
        in_specs=[vmem, vmem, vmem, hbm, hbm],
        out_specs=(hbm,) * 6,
        input_output_aliases={3: 0, 4: 1},
        scratch_shapes=[
            wide,
            pltpu.VMEM((3, 1, 512), F32),
            pltpu.VMEM((3, 512), F32),
            pltpu.SemaphoreType.DMA((6,)),
        ],
        compiler_params=pltpu.CompilerParams(vmem_limit_bytes=VMEM_BYTES),
        cost_estimate=cost,
    )(other, small, other_small, w_two, w_three)
    return (grad_coef, w_one, b_one[0], w_two, b_two[0], w_three, b_three[0])


def solution(mesh):
    fine = Mesh(mesh.devices.reshape(SIZES), AXES)
    fn, pts = ("xl", "y", "c"), ("xh", "z")
    return jax.shard_map(
        shards,
        mesh=fine,
        in_specs=(P(fn, pts), P(fn, None), P(None, pts), P(), P(), P(), P(), P(), P()),
        out_specs=(P(fn, pts), P(), P(), P(), P(), P(), P()),
        check_vma=False,
    )
```
